128 devices in a mesh: surf: 128 (over x, z, y, core).
Axes of the slice: x: 4, y: 4, z: 4, core: 2. Of those that a mesh axis runs over, the one named last changes fastest.
Arguments:
- signal: bfloat16 [16, 524288], P(None, 'surf'), may hold values from -6 to 6
- near_blocks: bfloat16 [2048, 8, 256, 256], P('surf'), may hold values from -0.375 to 0.375
- near_owner: int32 [2048, 8], P('surf'), may hold values from 0 to 127, as said below
- near_slot: int32 [2048, 8], P('surf'), may hold values from 0 to 15
- near_live: int32 [2048, 8], P('surf'), may hold values 0 or 1
- leaf_basis: bfloat16 [32, 524288], P(None, 'surf'), may hold values from -0.375 to 0.375
- transfer: float32 [2048, 1024], P('surf'), may hold values from -0.5 to 0.5
- leaf_coupling: float32 [2048, 32, 1024], P('surf'), may hold values from -0.1875 to 0.1875
- far_leaf: int32 [2048, 32], P('surf'), may hold values from 0 to 2047
- top_coupling: float32 [512, 32, 1024], P('surf'), may hold values from -0.1875 to 0.1875
- far_top: int32 [512, 32], P('surf'), may hold values from 0 to 511
Outputs:
- product: float32 [16, 524288], P(None, 'surf')
The draws below stay inside these ranges and needn't reach their ends.
Inputs may be any that keep to these rules, and one draw needn't show every extreme that they name: `near_owner`: the owner of a neighbour is at most 4 positions away, counted cyclically along surf, from the device that holds cluster c; every device has pairs at distance 4 on both sides.
All inputs are finite; a program needn't handle non-finite values. No bound on the sum of `near_live` on one device may be relied on, other than what follows from the above.
Results may differ from the reference program's by a relative error of at most 0.0003.
Values may be sent and summed in bfloat16 or wider, within the bound.
A program may use at most 128 MiB of HBM per device.

```python
import jax
import jax.numpy as jnp
from jax import lax

RHS = 16
LEAF = 256
R = 32
CL_DEV = 16
NEAR = 8
HOPS = 4
FARL = 32
FART = 32
BRANCH = 4
CLUSTERS = 2048
PANELS = 524288
PARENTS = 512
N_SURF = 128


def draw_near_owner(key, part):
    key = jax.random.fold_in(key, 11)
    key_offset, key_low, key_gap = jax.random.split(key, 3)
    per_device = CL_DEV * NEAR
    offsets = jax.random.randint(key_offset, (N_SURF, per_device), -HOPS, HOPS + 1)
    low_place = jax.random.randint(key_low, (N_SURF,), 0, per_device)
    high_place = (low_place + 1 + jax.random.randint(key_gap, (N_SURF,), 0, per_device - 1)) % per_device
    columns = jnp.arange(per_device, dtype=jnp.int32)[None, :]
    offsets = jnp.where(columns == low_place[:, None], -HOPS, offsets)
    offsets = jnp.where(columns == high_place[:, None], HOPS, offsets)
    owners = jnp.mod(jnp.arange(N_SURF, dtype=jnp.int32)[:, None] + offsets, N_SURF)
    return owners.reshape(CLUSTERS, NEAR).astype(jnp.int32)


def plant(drawn, key, least, high):
    shape = drawn.shape
    place = [jax.random.randint(jax.random.fold_in(key, axis), (), 0, shape[axis]) for axis in range(len(shape))]
    drawn = drawn.at[tuple(place)].set(least)
    longest = shape.index(max(shape))
    place[longest] = (place[longest] + 1) % shape[longest]
    return drawn.at[tuple(place)].set(high)


def level_of(key, extent, pieces, least, top_value):
    factor_of, own = 1.0, jax.random.fold_in(key, 6)
    for axis_at, blocks in pieces:
        steps = jnp.exp(jax.random.uniform(jax.random.fold_in(own, axis_at), (blocks,), jnp.float32, least / len(pieces), top_value / len(pieces)))
        factor_of = factor_of * jnp.repeat(steps, extent[axis_at] // blocks).reshape([-1 if axis == axis_at else 1 for axis in range(len(extent))])
    return factor_of


def scatter_about(stream_key, dims, width, most, cuts=(), held_as=jnp.bfloat16):
    level = level_of(stream_key, dims, cuts, -0.22, 0.18) if cuts else 1.0
    drawn = jax.random.normal(stream_key, dims, jnp.float32) * width * level
    return jnp.minimum(jnp.maximum(drawn, -most), most).astype(held_as)


def setup_inputs(seed: int = 0) -> dict:
    streams_of = jax.random.split(jax.random.key(seed), 12)
    return {
        "signal": scatter_about(streams_of[0], (RHS, PANELS), 1.0, 6.0, ((1, 128),)),
        "near_blocks": scatter_about(streams_of[1], (CLUSTERS, NEAR, LEAF, LEAF), LEAF ** -0.5, 0.375, ((0, 128),)),
        "near_owner": draw_near_owner(jax.random.fold_in(streams_of[11], 71), 0),
        "near_slot": plant(jax.random.randint(streams_of[3], (CLUSTERS, NEAR), 0, CL_DEV), jax.random.fold_in(streams_of[3], 1), 0, CL_DEV - 1).astype(jnp.int32),
        "near_live": plant((jax.random.randint(streams_of[4], (CLUSTERS, NEAR), 0, 8) < 7).astype(jnp.int32), jax.random.fold_in(streams_of[4], 1), 0, 1),
        "leaf_basis": scatter_about(streams_of[5], (R, PANELS), LEAF ** -0.5, 0.375, ((1, 128),)),
        "transfer": scatter_about(streams_of[6], (CLUSTERS, R * R), (R * BRANCH) ** -0.5, 0.5, ((0, 128),), jnp.float32),
        "leaf_coupling": scatter_about(streams_of[7], (CLUSTERS, FARL, R * R), (R * FARL) ** -0.5, 0.1875, ((0, 128),), jnp.float32),
        "far_leaf": plant(jax.random.randint(streams_of[8], (CLUSTERS, FARL), 0, CLUSTERS), jax.random.fold_in(streams_of[8], 1), 0, CLUSTERS - 1).astype(jnp.int32),
        "top_coupling": scatter_about(streams_of[9], (PARENTS, FART, R * R), (R * FART) ** -0.5, 0.1875, ((0, 128),), jnp.float32),
        "far_top": plant(jax.random.randint(streams_of[10], (PARENTS, FART), 0, PARENTS), jax.random.fold_in(streams_of[10], 1), 0, PARENTS - 1).astype(jnp.int32),
    }


exact_mode = lax.Precision.HIGHEST


def reference(signal, near_blocks, near_owner, near_slot, near_live, leaf_basis, transfer, leaf_coupling, far_leaf, top_coupling, far_top):
    panel_rows = signal.astype(jnp.float32).reshape(RHS, CLUSTERS, LEAF)
    global_id = (near_owner * CL_DEV + near_slot).astype(jnp.int32)
    live_mask = near_live.astype(jnp.float32)

    def near_step(accumulated, device_index):
        first_row = (device_index * CL_DEV).astype(jnp.int32)
        blocks = lax.dynamic_slice_in_dim(near_blocks, first_row, CL_DEV, 0).astype(jnp.float32)
        entry_ids = lax.dynamic_slice_in_dim(global_id, first_row, CL_DEV, 0)
        flags = lax.dynamic_slice_in_dim(live_mask, first_row, CL_DEV, 0)
        blocks = blocks * flags[:, :, None, None]
        own_rows = lax.dynamic_slice_in_dim(panel_rows, first_row, CL_DEV, 1)
        remote = jnp.take(panel_rows, entry_ids.reshape(-1), axis=1).reshape(RHS, CL_DEV, NEAR, LEAF)
        inward = jnp.einsum("qckb,ckab->qca", remote, blocks, precision=exact_mode)
        outward = jnp.einsum("qca,ckab->qckb", own_rows, blocks, precision=exact_mode)
        current = lax.dynamic_slice_in_dim(accumulated, first_row, CL_DEV, 1)
        accumulated = lax.dynamic_update_slice_in_dim(accumulated, current + inward, first_row, 1)
        accumulated = accumulated.at[:, entry_ids.reshape(-1), :].add(outward.reshape(RHS, CL_DEV * NEAR, LEAF))
        return accumulated, None

    near_total, _ = lax.scan(near_step, jnp.zeros((RHS, CLUSTERS, LEAF), jnp.float32), jnp.arange(N_SURF, dtype=jnp.int32))

    shapes = leaf_basis.astype(jnp.float32).reshape(R, CLUSTERS, LEAF)
    moments = jnp.einsum("rca,qca->crq", shapes, panel_rows, precision=exact_mode)
    picked = jnp.take(moments, far_leaf.reshape(-1), axis=0).reshape(CLUSTERS, FARL, R, RHS)
    leaf_field = jnp.einsum("ckrs,cksq->crq", leaf_coupling.reshape(CLUSTERS, FARL, R, R), picked, precision=exact_mode)
    lift_maps = transfer.reshape(PARENTS, BRANCH, R, R)
    upper_moments = jnp.einsum("pbrs,pbsq->prq", lift_maps, moments.reshape(PARENTS, BRANCH, R, RHS), precision=exact_mode)
    chosen = jnp.take(upper_moments, far_top.reshape(-1), axis=0).reshape(PARENTS, FART, R, RHS)
    top_field = jnp.einsum("pkrs,pksq->prq", top_coupling.reshape(PARENTS, FART, R, R), chosen, precision=exact_mode)
    downward = jnp.einsum("pbrs,prq->pbsq", lift_maps, top_field, precision=exact_mode).reshape(CLUSTERS, R, RHS)
    field = (leaf_field + downward).astype(jnp.bfloat16).astype(jnp.float32)
    far_part = jnp.einsum("crq,rca->qca", field, shapes, precision=exact_mode)
    return (near_total + far_part).reshape(RHS, PANELS)
```

```python
import jax
import jax.numpy as jnp
from jax import lax
from jax.experimental import pallas as pl
from jax.experimental.pallas import tpu as pltpu
from jax.sharding import PartitionSpec as P

HOPS = 4
OFFS = 2 * HOPS + 1
CHUNKS = 2
MESH = pl.DeviceIdType.MESH
F32 = jnp.float32
BF16 = jnp.bfloat16
NT = (((1,), (1,)), ((), ()))


def split(value):
    high = value.astype(BF16)
    return high, (value - high.astype(F32)).astype(BF16)


def dot_two(value, matrix, dims=(((1,), (0,)), ((), ()))):
    high, low = split(value)
    return lax.dot_general(high, matrix, dims, preferred_element_type=F32) + lax.dot_general(
        low, matrix, dims, preferred_element_type=F32
    )


def kernel(
    owner_ref,
    slot_ref,
    live_ref,
    far_leaf_ref,
    far_top_ref,
    signal_ref,
    basis_ref,
    transfer_ref,
    near_hbm,
    leaf_hbm,
    top_hbm,
    out_ref,
    near_buf,
    leaf_buf,
    top_buf,
    window,
    outgoing,
    hot_rows,
    hot,
    even_terms,
    odd_terms,
    partner_terms,
    far_terms,
    back_terms,
    table,
    sum_blocks,
    sum_children,
    leaf_acc,
    down_acc,
    near_sem,
    coup_sem,
    sig_send,
    sig_recv,
    ret_send,
    ret_recv,
    tab_send,
    tab_recv,
    par_send,
    par_recv,
):
    rhs = 16
    leaf = 256
    clusters = 16
    near = 8
    n = 128
    me = lax.axis_index("surf")
    core = lax.rem(me, 2)
    y = lax.rem(me // 2, 4)
    z = lax.rem(me // 8, 4)
    x = me // 32

    def at(px, pz, py):
        return ((px * 4 + pz) * 4 + py) * 2 + core

    def turn(value, step):
        return lax.rem(value + step + 4, 4)

    partner = me + 1 - 2 * core
    ahead = lax.rem(me + 2, n)
    behind = lax.rem(me + n - 2, n)
    y_up, y_down = at(x, z, turn(y, 1)), at(x, z, turn(y, -1))
    z_up, z_down = at(x, turn(z, 1), y), at(x, turn(z, -1), y)
    x_up, x_down = at(turn(x, 1), z, y), at(turn(x, -1), z, y)

    near_in = []
    for c in range(clusters):
        near_in.append(pltpu.make_async_copy(near_hbm.at[c], near_buf.at[c], near_sem.at[c]))
    leaf_in = pltpu.make_async_copy(leaf_hbm, leaf_buf, coup_sem.at[0])
    top_in = pltpu.make_async_copy(top_hbm, top_buf, coup_sem.at[1])
    for copy in near_in:
        copy.start()
    leaf_in.start()
    top_in.start()

    barrier = pltpu.get_barrier_semaphore()
    for peer in (partner, ahead, behind, y_up, y_down, z_up, z_down, x_up, x_down):
        pl.semaphore_signal(barrier, inc=1, device_id=(peer,), device_id_type=MESH)

    for c in range(clusters):
        window[HOPS * clusters + c] = signal_ref[:, c * leaf : (c + 1) * leaf]

    group = lax.broadcasted_iota(jnp.int32, (rhs, 128), 1) // 32
    row_id = lax.broadcasted_iota(jnp.int32, (1024, 128), 0)
    lane_id = lax.broadcasted_iota(jnp.int32, (1024, 128), 1)
    sum_blocks[...] = (row_id // 32 == lane_id % 32).astype(F32).astype(BF16)
    sum_children[...] = (row_id % 32 == lane_id).astype(F32).astype(BF16)

    @pl.loop(0, 4, init_carry=jnp.zeros((rhs, 128), F32))
    def upper_rows(p, upper):
        packed = jnp.zeros((rhs, 128), F32)
        lifted = [jnp.zeros((rhs, 128), F32) for _ in range(8)]
        for b in range(4):
            c = p * 4 + b
            columns = pl.ds(pl.multiple_of(c * leaf, leaf), leaf)
            shape = basis_ref[:, columns]
            moment = lax.dot_general(
                signal_ref[:, columns],
                jnp.concatenate([shape] * 4, axis=0),
                NT,
                preferred_element_type=F32,
            )
            packed = jnp.where(group == b, moment, packed)
            lift = transfer_ref[pl.ds(c, 1), :]
            lifted = [a + moment * lift[:, g * 128 : (g + 1) * 128] for g, a in enumerate(lifted)]
        table[x, z, y, core, p] = packed
        total = dot_two(jnp.concatenate(lifted, axis=1), sum_blocks[...])
        return jnp.where(group == p, total, upper)

    table[x, z, y, core, 4] = upper_rows

    pl.semaphore_wait(barrier, 9)

    def remote(src, dst, send, recv, device):
        return pltpu.make_async_remote_copy(
            src_ref=src,
            dst_ref=dst,
            send_sem=send,
            recv_sem=recv,
            device_id=(device,),
            device_id_type=MESH,
        )

    sent = []

    def start(copy):
        copy.start()
        sent.append(copy)
        return copy

    def place(offset):
        return window.at[pl.ds(offset * clusters, clusters)]

    def sig(src, dst, index, device):
        return start(remote(place(src), place(dst), sig_send.at[index], sig_recv.at[index], device))

    from_behind = sig(4, 2, 0, ahead)
    from_ahead = sig(4, 6, 1, behind)

    def tab(src, index, device):
        return start(remote(src, src, tab_send.at[index], tab_recv.at[index], device))

    own = table.at[x, z, y, core]
    y_from = [tab(own, 0, y_up), tab(own, 1, y_down)]

    def forward_y():
        for copy in y_from:
            copy.wait_recv()
        return [
            tab(table.at[x, z, turn(y, -1), core, pl.ds(0, 3)], 2, y_up),
            tab(table.at[x, z, turn(y, 1), core, pl.ds(3, 2)], 3, y_down),
        ]

    def par(src, index):
        return start(remote(src, src, par_send.at[index], par_recv.at[index], partner))

    lower, higher = pl.ds(0, 2), pl.ds(2, 2)

    def first_legs(copies):
        for copy in copies:
            copy.wait_recv()
        a = table.at[x, z, lower, core]
        b = table.at[x, z, higher, core]
        return [tab(a, 4, x_up), tab(a, 5, x_down), tab(b, 6, z_up), tab(b, 7, z_down)]

    def first_forwards(copies):
        for copy in copies:
            copy.wait_recv()
        return [
            tab(table.at[turn(x, -1), z, 0, core], 8, x_up),
            tab(table.at[turn(x, 1), z, 1, core], 9, x_down),
            tab(table.at[x, turn(z, -1), 2, core], 10, z_up),
            tab(table.at[x, turn(z, 1), 3, core], 11, z_down),
        ]

    def second_legs(copies):
        for copy in copies:
            copy.wait_recv()
        a = table.at[:, z, lower, core]
        b = table.at[x, :, higher, core]
        return [tab(a, 12, z_up), tab(a, 13, z_down), tab(b, 14, x_up), tab(b, 15, x_down)] + [
            par(a, 0),
            par(b, 1),
        ]

    def second_forwards(copies):
        for copy in copies[:4]:
            copy.wait_recv()
        more = [
            tab(table.at[:, turn(z, -1), 0, core], 16, z_up),
            tab(table.at[:, turn(z, 1), 1, core], 17, z_down),
            tab(table.at[turn(x, -1), :, 2, core], 18, x_up),
            tab(table.at[turn(x, 1), :, 3, core], 19, x_down),
        ]
        more += [
            par(table.at[:, turn(z, -1), lower, core], 2),
            par(table.at[:, turn(z, 1), lower, core], 3),
            par(table.at[turn(x, -1), :, higher, core], 4),
            par(table.at[turn(x, 1), :, higher, core], 5),
        ]
        return copies[4:] + more

    def last_pairs(copies):
        for copy in copies[2:6]:
            copy.wait_recv()
        return copies[:2] + copies[6:] + [
            par(table.at[:, turn(z, 2), lower, core], 6),
            par(table.at[turn(x, 2), :, higher, core], 7),
        ]

    window_row = lax.broadcasted_iota(jnp.int32, (1, 256), 1)

    def place_of(c, k):
        offset = lax.rem(owner_ref[c, k] - me + (HOPS + n), n)
        return jnp.minimum(offset, OFFS - 1) * clusters + slot_ref[c, k]

    def outward(first, count):
        for copy in near_in[first : first + count]:
            copy.wait()

        @pl.loop(first, first + count)
        def _(c):
            here = signal_ref[:, pl.ds(pl.multiple_of(c * leaf, leaf), leaf)]
            for k in range(near):
                rows = pl.ds(pl.multiple_of((c * near + k) * rhs, rhs), rhs)
                term = jnp.dot(here, near_buf[c, k], preferred_element_type=F32)
                outgoing[0, rows, :] = term[:, :128]
                outgoing[1, rows, :] = term[:, 128:]
                target = place_of(c, k) + (1 - live_ref[c, k]) * 256
                hot_rows[pl.ds(c * near + k, 1), :] = jnp.where(window_row == target, 1.0, 0.0)

    def scatter(first, count):
        @pl.loop(first, first + count)
        def _(q):
            picks = pl.ds(q, clusters * near, stride=rhs)
            terms = jnp.concatenate([outgoing[0, picks, :], outgoing[1, picks, :]], axis=1)
            high, low = split(terms)
            summed = jnp.dot(
                hot[...], jnp.concatenate([high, low], axis=0), preferred_element_type=F32
            )
            rows = pl.ds(pl.multiple_of(q * clusters, clusters), clusters)
            for offset in range(OFFS):
                terms_ref = odd_terms if offset % 2 else even_terms
                block = summed[offset * clusters : (offset + 1) * clusters, :]
                terms_ref[offset // 2, 0, rows, :] = block[:, :128]
                terms_ref[offset // 2, 1, rows, :] = block[:, 128:]

    height = rhs * clusters // CHUNKS

    def part(h):
        return pl.ds(h * height, height)

    def ret(src, dst, index, device):
        return start(remote(src, dst, ret_send.at[index], ret_recv.at[index], device))

    def to_partner(h):
        return ret(odd_terms.at[:, :, part(h)], partner_terms.at[:, :, part(h)], 5 * h, partner)

    def to_far(h, copy):
        copy.wait_recv()
        rows = part(h)
        for i in range(4):
            slot = i + 1 - core
            even_terms[slot, :, rows, :] = even_terms[slot, :, rows, :] + partner_terms[i, :, rows, :]
        return [
            ret(even_terms.at[4, :, rows], far_terms.at[0, :, rows], 5 * h + 1, ahead),
            ret(even_terms.at[0, :, rows], far_terms.at[1, :, rows], 5 * h + 2, behind),
        ]

    def to_next(h, copies):
        rows = part(h)
        copies[0].wait_recv()
        even_terms[3, :, rows, :] = even_terms[3, :, rows, :] + far_terms[0, :, rows, :]
        up = ret(even_terms.at[3, :, rows], back_terms.at[0, :, rows], 5 * h + 3, ahead)
        copies[1].wait_recv()
        even_terms[1, :, rows, :] = even_terms[1, :, rows, :] + far_terms[1, :, rows, :]
        down = ret(even_terms.at[1, :, rows], back_terms.at[1, :, rows], 5 * h + 4, behind)
        return [up, down]

    def inward(first, count):
        @pl.loop(first, first + count)
        def _(c):
            total = jnp.zeros((rhs, leaf), F32)
            for k in range(near):
                there = window[place_of(c, k)]
                there = (there.astype(F32) * live_ref[c, k].astype(F32)).astype(BF16)
                total = total + lax.dot_general(
                    there, near_buf[c, k], NT, preferred_element_type=F32
                )
            out_ref[:, pl.ds(pl.multiple_of(c * leaf, leaf), leaf)] = total

    def picked(device, block, quarter):
        tile = table[device >> 5, (device >> 3) & 3, (device >> 1) & 3, device & 1, block]
        tile = jnp.where(group == quarter, tile, 0.0)
        tile = tile + pltpu.roll(tile, 32, 1)
        return tile + pltpu.roll(tile, 64, 1)

    def coupled(buf, row, pick):
        def step(k, sums):
            tile = pick(k)
            factors = buf[row, pl.ds(k, 1), :]
            return tuple(
                a + tile * factors[:, g * 128 : (g + 1) * 128] for g, a in enumerate(sums)
            )

        sums = lax.fori_loop(
            0, 32, step, tuple(jnp.zeros((rhs, 128), F32) for _ in range(8)), unroll=4
        )
        return jnp.concatenate(sums, axis=1)

    def far(first, count):
        @pl.loop(first, first + count)
        def _(p):
            def pick_top(k):
                j = far_top_ref[p, k]
                return picked(j >> 2, 4, j & 3)

            top = dot_two(coupled(top_buf, p, pick_top), sum_blocks[...])[:, :32]
            spread = dot_two(top, sum_blocks[:, :32], NT)

            @pl.loop(0, 4)
            def _(b):
                c = p * 4 + b

                def pick_leaf(k):
                    j = far_leaf_ref[c, k]
                    return picked(j >> 4, (j >> 2) & 3, j & 3)

                rows = pl.ds(pl.multiple_of(b * rhs, rhs), rhs)
                leaf_acc[rows, :] = coupled(leaf_buf, c, pick_leaf)
                down_acc[rows, :] = spread * transfer_ref[pl.ds(c, 1), :]

            field = dot_two(leaf_acc[...], sum_blocks[...]) + dot_two(
                down_acc[...], sum_children[...]
            )
            field = field[:, :32].astype(BF16)
            for b in range(4):
                columns = pl.ds(pl.multiple_of((p * 4 + b) * leaf, leaf), leaf)
                out_ref[:, columns] = out_ref[:, columns] + jnp.dot(
                    field[b * rhs : (b + 1) * rhs], basis_ref[:, columns], preferred_element_type=F32
                )

    own_to_partner = sig(4, 3 + 2 * core, 2, partner)
    outward(0, 2)
    y_more = forward_y()
    outward(2, 4)
    from_behind.wait_recv()
    from_ahead.wait_recv()
    second_behind = sig(2, 0, 3, ahead)
    second_ahead = sig(6, 8, 4, behind)
    near_pairs = [
        sig(2, 1 + 2 * core, 5, partner),
        sig(6, 5 + 2 * core, 6, partner),
    ]
    legs = first_legs(y_more)
    outward(6, 4)
    legs = first_forwards(legs)
    outward(10, 6)
    legs = second_legs(legs)
    second_behind.wait_recv()
    second_ahead.wait_recv()
    last_pair = sig(8 - 8 * core, 7 - 6 * core, 7, partner)
    flipped = hot_rows[...].T.astype(BF16)
    hot[...] = jnp.concatenate([flipped, flipped], axis=1)[: OFFS * clusters, :]
    stage = []
    for h in range(CHUNKS):
        scatter(h * rhs // CHUNKS, rhs // CHUNKS)
        stage.append(to_partner(h))
    for copy in [own_to_partner, last_pair] + near_pairs:
        copy.wait_recv()
    legs = second_forwards(legs)
    inward(0, 4)
    stage = [to_far(h, copy) for h, copy in enumerate(stage)]
    inward(4, 4)
    legs = last_pairs(legs)
    inward(8, 8)
    stage = [to_next(h, copies) for h, copies in enumerate(stage)]
    leaf_in.wait()
    top_in.wait()
    for copy in legs:
        copy.wait_recv()
    far(0, 4)
    for copies in stage:
        for copy in copies:
            copy.wait_recv()

    @pl.loop(0, clusters)
    def _(c):
        rows = pl.ds(c, rhs, stride=clusters)
        for half in range(2):
            columns = pl.ds(pl.multiple_of(c * leaf + half * 128, 128), 128)
            total = out_ref[:, columns] + even_terms[2, half, rows, :]
            out_ref[:, columns] = (
                total + back_terms[0, half, rows, :] + back_terms[1, half, rows, :]
            )

    for copy in sent:
        copy.wait_send()


def shards(
    signal,
    near_blocks,
    near_owner,
    near_slot,
    near_live,
    leaf_basis,
    transfer,
    leaf_coupling,
    far_leaf,
    top_coupling,
    far_top,
):
    smem = pl.BlockSpec(memory_space=pltpu.SMEM)
    vmem = pl.BlockSpec(memory_space=pltpu.VMEM)
    hbm = pl.BlockSpec(memory_space=pl.ANY)
    dma = pltpu.SemaphoreType.DMA
    return pl.pallas_call(
        kernel,
        out_shape=jax.ShapeDtypeStruct((16, 4096), F32),
        in_specs=[smem] * 5 + [vmem] * 3 + [hbm] * 3,
        out_specs=vmem,
        scratch_shapes=[
            pltpu.VMEM((16, 8, 256, 256), BF16),
            pltpu.VMEM((16, 32, 1024), F32),
            pltpu.VMEM((4, 32, 1024), F32),
            pltpu.VMEM((OFFS * 16, 16, 256), BF16),
            pltpu.VMEM((2, 2048, 128), F32),
            pltpu.VMEM((128, 256), F32),
            pltpu.VMEM((OFFS * 16, 256), BF16),
            pltpu.VMEM((5, 2, 256, 128), F32),
            pltpu.VMEM((4, 2, 256, 128), F32),
            pltpu.VMEM((4, 2, 256, 128), F32),
            pltpu.VMEM((2, 2, 256, 128), F32),
            pltpu.VMEM((2, 2, 256, 128), F32),
            pltpu.VMEM((4, 4, 4, 2, 5, 16, 128), F32),
            pltpu.VMEM((1024, 128), BF16),
            pltpu.VMEM((1024, 128), BF16),
            pltpu.VMEM((64, 1024), F32),
            pltpu.VMEM((64, 1024), F32),
            dma((16,)),
            dma((2,)),
            dma((8,)),
            dma((8,)),
            dma((5 * CHUNKS,)),
            dma((5 * CHUNKS,)),
            dma((20,)),
            dma((20,)),
            dma((8,)),
            dma((8,)),
        ],
        compiler_params=pltpu.CompilerParams(
            collective_id=0, has_side_effects=True, vmem_limit_bytes=52 * 1024 * 1024
        ),
        cost_estimate=pl.CostEstimate(
            flops=1200000000, bytes_accessed=20000000, transcendentals=0
        ),
    )(
        near_owner,
        near_slot,
        near_live,
        far_leaf,
        far_top,
        signal,
        leaf_basis,
        transfer,
        near_blocks,
        leaf_coupling,
        top_coupling,
    )


def solution(mesh):
    placed = (
        P(None, "surf"),
        P("surf", None, None, None),
        P("surf", None),
        P("surf", None),
        P("surf", None),
        P(None, "surf"),
        P("surf", None),
        P("surf", None, None),
        P("surf", None),
        P("surf", None, None),
        P("surf", None),
    )
    return jax.shard_map(
        shards, mesh=mesh, in_specs=placed, out_specs=P(None, "surf"), check_vma=False
    )
```

```python
import jax
import jax.numpy as jnp
from jax import lax
from jax.experimental import pallas as pl
from jax.experimental.pallas import tpu as pltpu
from jax.sharding import PartitionSpec as P

HOPS = 4
OFFS = 2 * HOPS + 1
LEAST = -24.0
STEPS = 800.0
MESH = pl.DeviceIdType.MESH
F32 = jnp.float32
BF16 = jnp.bfloat16
NT = (((1,), (1,)), ((), ()))


def split(value):
    high = value.astype(BF16)
    return high, (value - high.astype(F32)).astype(BF16)


def dot_two(value, matrix, dims=(((1,), (0,)), ((), ()))):
    high, low = split(value)
    return lax.dot_general(high, matrix, dims, preferred_element_type=F32) + lax.dot_general(
        low, matrix, dims, preferred_element_type=F32
    )


def encode(value):
    level = (jnp.log2(jnp.maximum(jnp.abs(value), 2.0**LEAST)) - LEAST) * STEPS
    level = jnp.round(jnp.minimum(level, 32767.0))
    return jnp.where(value < 0, -level, level).astype(jnp.int32).astype(jnp.int16)


def decode(level):
    size = jnp.exp2(jnp.abs(level) * (1.0 / STEPS) + LEAST)
    return jnp.where(level < 0, -size, jnp.where(level > 0, size, 0.0))


def kernel(
    owner_hbm,
    slot_hbm,
    live_hbm,
    far_leaf_hbm,
    far_top_hbm,
    signal_hbm,
    basis_hbm,
    transfer_hbm,
    near_hbm,
    leaf_hbm,
    top_hbm,
    out_ref,
    owner_ref,
    slot_ref,
    live_ref,
    far_leaf_ref,
    far_top_ref,
    signal_ref,
    basis_ref,
    transfer_ref,
    near_buf,
    leaf_buf,
    top_buf,
    window,
    outgoing,
    hot_rows,
    hot,
    even_terms,
    odd_terms,
    partner_terms,
    codes_out,
    codes_in,
    table,
    tiles,
    sum_blocks,
    sum_children,
    leaf_acc,
    down_acc,
    near_sem,
    load_sem,
    sig_send,
    sig_recv,
    ret_send,
    ret_recv,
    tab_send,
    tab_recv,
    par_send,
    par_recv,
):
    rhs = 16
    leaf = 256
    clusters = 16
    near = 8
    n = 128
    me = lax.axis_index("surf")
    core = lax.rem(me, 2)
    y = lax.rem(me // 2, 4)
    z = lax.rem(me // 8, 4)
    x = me // 32

    def at(px, pz, py):
        return ((px * 4 + pz) * 4 + py) * 2 + core

    def turn(value, step):
        return lax.rem(value + step + 4, 4)

    def along(step):
        return lax.rem(me + step + n, n)

    partner = me + 1 - 2 * core
    steps = (1, -1, 2)
    y_peers = [at(x, z, turn(y, step)) for step in steps]
    z_peers = [at(x, turn(z, step), y) for step in steps]
    x_peers = [at(turn(x, step), z, y) for step in steps]
    surf_peers = [along(step) for step in (-4, -2, 2, 4)]

    loads = [
        pltpu.make_async_copy(src, dst, load_sem.at[i])
        for i, (src, dst) in enumerate(
            (
                (signal_hbm, signal_ref),
                (basis_hbm, basis_ref),
                (transfer_hbm, transfer_ref),
                (owner_hbm, owner_ref),
                (slot_hbm, slot_ref),
                (live_hbm, live_ref),
                (far_leaf_hbm, far_leaf_ref),
                (far_top_hbm, far_top_ref),
                (leaf_hbm, leaf_buf),
                (top_hbm, top_buf),
            )
        )
    ]
    near_in = [
        pltpu.make_async_copy(near_hbm.at[c], near_buf.at[c], near_sem.at[c])
        for c in range(clusters)
    ]
    for copy in loads[:3]:
        copy.start()
    barrier = pltpu.get_barrier_semaphore()
    peers = [partner] + surf_peers + y_peers + z_peers + x_peers
    for peer in peers:
        pl.semaphore_signal(barrier, inc=1, device_id=(peer,), device_id_type=MESH)
    for copy in loads[3:8] + near_in + loads[8:]:
        copy.start()

    group = lax.broadcasted_iota(jnp.int32, (rhs, 128), 1) // 32
    row_id = lax.broadcasted_iota(jnp.int32, (1024, 128), 0)
    lane_id = lax.broadcasted_iota(jnp.int32, (1024, 128), 1)
    sum_blocks[...] = (row_id // 32 == lane_id % 32).astype(F32).astype(BF16)
    sum_children[...] = (row_id % 32 == lane_id % 32).astype(F32).astype(BF16)

    loads[0].wait()
    for c in range(clusters):
        window[HOPS * clusters + c] = signal_ref[:, c * leaf : (c + 1) * leaf]
    loads[1].wait()
    loads[2].wait()

    upper = jnp.zeros((rhs, 128), F32)
    for p in range(4):
        packed = jnp.zeros((rhs, 128), F32)
        lifted = [jnp.zeros((rhs, 128), F32) for _ in range(8)]
        for b in range(4):
            c = p * 4 + b
            columns = slice(c * leaf, (c + 1) * leaf)
            shape = basis_ref[:, columns]
            moment = lax.dot_general(
                signal_ref[:, columns],
                jnp.concatenate([shape] * 4, axis=0),
                NT,
                preferred_element_type=F32,
            )
            packed = jnp.where(group == b, moment, packed)
            lift = transfer_ref[c : c + 1, :]
            lifted = [a + moment * lift[:, g * 128 : (g + 1) * 128] for g, a in enumerate(lifted)]
        table[x, z, y, core, p] = encode(packed)
        total = dot_two(jnp.concatenate(lifted, axis=1), sum_blocks[...])
        upper = jnp.where(group == p, total, upper)
    table[x, z, y, core, 4] = encode(upper)

    pl.semaphore_wait(barrier, len(peers))

    def remote(src, dst, send, recv, device):
        return pltpu.make_async_remote_copy(
            src_ref=src,
            dst_ref=dst,
            send_sem=send,
            recv_sem=recv,
            device_id=(device,),
            device_id_type=MESH,
        )

    sent = []

    def start(copy):
        copy.start()
        sent.append(copy)
        return copy

    def arrived(copies):
        for copy in copies:
            copy.wait_recv()

    def tab(src, index, device):
        return start(remote(src, src, tab_send.at[index], tab_recv.at[index], device))

    def par(src, index):
        return start(remote(src, src, par_send.at[index], par_recv.at[index], partner))

    def place(offset):
        return window.at[pl.ds(offset * clusters, clusters)]

    def sig(src, dst, index, device):
        return start(remote(place(src), place(dst), sig_send.at[index], sig_recv.at[index], device))

    def rows_along_y():
        own = table.at[x, z, y, core]
        return [tab(own, i, peer) for i, peer in enumerate(y_peers)]

    def rows_out(copies):
        arrived(copies)
        row = table.at[x, z, :, core]
        return [tab(row, 3 + i, peer) for i, peer in enumerate(x_peers)] + [
            tab(row, 6 + i, peer) for i, peer in enumerate(z_peers)
        ]

    def halves_out(copies):
        more = []
        for i, step in enumerate(steps):
            copies[i].wait_recv()
            half = table.at[turn(x, -step), z, pl.ds(0, 2), core]
            more += [tab(half, 9 + 3 * i + j, peer) for j, peer in enumerate(z_peers)]
            copies[3 + i].wait_recv()
            half = table.at[x, turn(z, -step), pl.ds(2, 2), core]
            more += [tab(half, 18 + 3 * i + j, peer) for j, peer in enumerate(x_peers)]
        return more + [par(table.at[:, z, :, core], 0)]

    def to_other_core(copies):
        for j, step in enumerate(steps):
            arrived([copies[6 * i + j] for i in range(3)])
            arrived([copies[6 * j + 3 + i] for i in range(3)])
            copies.append(par(table.at[:, turn(z, -step), :, core], 1 + j))
        return copies[18:]

    window_row = lax.broadcasted_iota(jnp.int32, (1, 256), 1)

    def place_of(c, k):
        offset = lax.rem(owner_ref[k, c] - me + (HOPS + n), n)
        return jnp.minimum(offset, OFFS - 1) * clusters + slot_ref[k, c]

    def outward(first, count):
        for copy in near_in[first : first + count]:
            copy.wait()

        @pl.loop(first, first + count)
        def _(c):
            here = signal_ref[:, pl.ds(pl.multiple_of(c * leaf, leaf), leaf)]
            for k in range(near):
                rows = pl.ds(pl.multiple_of((c * near + k) * rhs, rhs), rhs)
                term = jnp.dot(here, near_buf[c, k], preferred_element_type=F32)
                outgoing[0, rows, :] = term[:, :128]
                outgoing[1, rows, :] = term[:, 128:]
                target = place_of(c, k) + (1 - live_ref[k, c]) * 256
                hot_rows[pl.ds(c * near + k, 1), :] = jnp.where(window_row == target, 1.0, 0.0)

    def scatter(half):
        @pl.loop(0, rhs // 2)
        def _(pair):
            terms = jnp.concatenate(
                [
                    outgoing[half, pl.ds(pair * 2 + i, clusters * near, stride=rhs), :]
                    for i in range(2)
                ],
                axis=1,
            )
            high, low = split(terms)
            summed = jnp.dot(
                hot[...], jnp.concatenate([high, low], axis=0), preferred_element_type=F32
            )
            for i in range(2):
                rows = pl.ds(pl.multiple_of((pair * 2 + i) * clusters, clusters), clusters)
                for offset in range(OFFS):
                    terms_ref = odd_terms if offset % 2 else even_terms
                    terms_ref[offset // 2, half, rows, :] = summed[
                        offset * clusters : (offset + 1) * clusters, i * 128 : (i + 1) * 128
                    ]

    def ret(src, dst, index, device):
        return start(remote(src, dst, ret_send.at[index], ret_recv.at[index], device))

    def to_partner(half):
        return ret(odd_terms.at[:, half], partner_terms.at[:, half], 5 * half, partner)

    height = rhs * clusters

    def to_targets(half, copy):
        copy.wait_recv()
        copies = []
        for i, offset in enumerate((0, 1, 3, 4)):
            j = offset - 1 + core
            valid = jnp.logical_and(j >= 0, j <= 3)
            weight = jnp.where(valid, 1.0, 0.0)
            summed = (
                even_terms[offset, half]
                + partner_terms[jnp.clip(j, 0, 3), half] * weight
            )
            peak = jnp.maximum(jnp.max(jnp.abs(summed), keepdims=True), 2.0**-100)
            power = jnp.ceil(jnp.log2(peak * (1.0 / 32000.0)))
            codes_out[i, half, :height] = (
                jnp.round(summed * jnp.exp2(-power)).astype(jnp.int32).astype(jnp.int16)
            )
            codes_out[i, half, height:] = (
                jnp.broadcast_to(power, (16, 128)).astype(jnp.int32).astype(jnp.int16)
            )
            copies.append(
                ret(codes_out.at[i, half], codes_in.at[i, half], 5 * half + 1 + i, surf_peers[i])
            )
        even_terms[2, half] = even_terms[2, half] + partner_terms[1 + core, half]
        return copies

    def add_returned(half, copies):
        total = even_terms[2, half]
        for i, copy in enumerate(copies):
            copy.wait_recv()
            power = codes_in[i, half, height:].astype(jnp.int32).astype(F32)[:1]
            total = total + codes_in[i, half, :height].astype(jnp.int32).astype(F32) * jnp.exp2(
                power
            )
        even_terms[2, half] = total

    def inward(first, count):
        @pl.loop(first, first + count)
        def _(c):
            total = jnp.zeros((rhs, leaf), F32)
            for k in range(near):
                there = window[place_of(c, k)]
                there = (there.astype(F32) * live_ref[k, c].astype(F32)).astype(BF16)
                total = total + lax.dot_general(
                    there, near_buf[c, k], NT, preferred_element_type=F32
                )
            out_ref[:, pl.ds(pl.multiple_of(c * leaf, leaf), leaf)] = total

    def picked(device, block, quarter):
        tile = table[device >> 5, (device >> 3) & 3, (device >> 1) & 3, device & 1, block]
        level = tile.astype(jnp.int32).astype(F32)
        return split(decode(jnp.where(group == quarter, level, 0.0)))

    def coupled(buf, row, pick):
        for first in (0, 16):
            pairs = [pick(first + k) for k in range(16)]
            both = jnp.concatenate(
                [jnp.concatenate([pair[i] for pair in pairs], axis=0) for i in range(2)], axis=1
            )
            tiles[first * rhs : (first + 16) * rhs, :] = jnp.dot(
                both, sum_children[:256, :], preferred_element_type=F32
            )

        def step(eight, sums):
            factors = buf[row, pl.ds(pl.multiple_of(eight * 8, 8), 8), :]
            for k in range(8):
                tile = tiles[pl.ds(pl.multiple_of((eight * 8 + k) * rhs, rhs), rhs), :]
                sums = tuple(
                    a + tile * factors[k : k + 1, g * 128 : (g + 1) * 128]
                    for g, a in enumerate(sums)
                )
            return sums

        sums = lax.fori_loop(0, 4, step, tuple(jnp.zeros((rhs, 128), F32) for _ in range(8)))
        return jnp.concatenate(sums, axis=1)

    def far(first, count):
        @pl.loop(first, first + count)
        def _(p):
            def pick_top(k):
                j = far_top_ref[p, k]
                return picked(j >> 2, 4, j & 3)

            top = dot_two(coupled(top_buf, p, pick_top), sum_blocks[...])[:, :32]
            spread = dot_two(top, sum_blocks[:, :32], NT)

            @pl.loop(0, 4)
            def _(b):
                c = p * 4 + b

                def pick_leaf(k):
                    j = far_leaf_ref[c, k]
                    return picked(j >> 4, (j >> 2) & 3, j & 3)

                rows = pl.ds(pl.multiple_of(b * rhs, rhs), rhs)
                leaf_acc[rows, :] = coupled(leaf_buf, c, pick_leaf)
                down_acc[rows, :] = spread * transfer_ref[pl.ds(c, 1), :]

            field = dot_two(leaf_acc[...], sum_blocks[...]) + dot_two(
                down_acc[...], sum_children[...]
            )
            field = field[:, :32].astype(BF16)
            for b in range(4):
                columns = pl.ds(pl.multiple_of((p * 4 + b) * leaf, leaf), leaf)
                out_ref[:, columns] = out_ref[:, columns] + jnp.dot(
                    field[b * rhs : (b + 1) * rhs], basis_ref[:, columns], preferred_element_type=F32
                )

    legs = rows_along_y()
    signals = [
        sig(4, 8, 0, surf_peers[0]),
        sig(4, 6, 1, surf_peers[1]),
        sig(4, 2, 2, surf_peers[2]),
        sig(4, 0, 3, surf_peers[3]),
    ]
    pairs = [sig(4, 3 + 2 * core, 4, partner)]
    for copy in loads[3:6]:
        copy.wait()
    outward(0, 5)
    legs = rows_out(legs)
    outward(5, 11)
    flipped = hot_rows[...].T.astype(BF16)
    hot[...] = jnp.concatenate([flipped, flipped], axis=1)[: OFFS * clusters, :]
    scatter(0)
    stage = [to_partner(0)]
    scatter(1)
    stage.append(to_partner(1))
    legs = halves_out(legs)
    arrived(signals)
    pairs += [
        sig(2, 1 + 2 * core, 5, partner),
        sig(6, 5 + 2 * core, 6, partner),
        sig(8 - 8 * core, 7 - 6 * core, 7, partner),
    ]
    stage = [to_targets(half, copy) for half, copy in enumerate(stage)]
    arrived(pairs)
    inward(0, 12)
    legs = to_other_core(legs)
    inward(12, 4)
    for copy in loads[6:]:
        copy.wait()
    arrived(legs)
    far(0, 4)
    for half, copies in enumerate(stage):
        add_returned(half, copies)

    @pl.loop(0, clusters)
    def _(c):
        rows = pl.ds(c, rhs, stride=clusters)
        for half in range(2):
            columns = pl.ds(pl.multiple_of(c * leaf + half * 128, 128), 128)
            out_ref[:, columns] = out_ref[:, columns] + even_terms[2, half, rows, :]

    for copy in sent:
        copy.wait_send()


def shards(
    signal,
    near_blocks,
    near_owner,
    near_slot,
    near_live,
    leaf_basis,
    transfer,
    leaf_coupling,
    far_leaf,
    top_coupling,
    far_top,
):
    hbm = pl.BlockSpec(memory_space=pl.ANY)
    dma = pltpu.SemaphoreType.DMA
    return pl.pallas_call(
        kernel,
        out_shape=jax.ShapeDtypeStruct((16, 4096), F32),
        in_specs=[hbm] * 11,
        out_specs=pl.BlockSpec(memory_space=pltpu.VMEM),
        scratch_shapes=[
            pltpu.SMEM((8, 16), jnp.int32),
            pltpu.SMEM((8, 16), jnp.int32),
            pltpu.SMEM((8, 16), jnp.int32),
            pltpu.SMEM((16, 32), jnp.int32),
            pltpu.SMEM((4, 32), jnp.int32),
            pltpu.VMEM((16, 4096), BF16),
            pltpu.VMEM((32, 4096), BF16),
            pltpu.VMEM((16, 1024), F32),
            pltpu.VMEM((16, 8, 256, 256), BF16),
            pltpu.VMEM((16, 32, 1024), F32),
            pltpu.VMEM((4, 32, 1024), F32),
            pltpu.VMEM((OFFS * 16, 16, 256), BF16),
            pltpu.VMEM((2, 2048, 128), F32),
            pltpu.VMEM((128, 256), F32),
            pltpu.VMEM((OFFS * 16, 256), BF16),
            pltpu.VMEM((5, 2, 256, 128), F32),
            pltpu.VMEM((4, 2, 256, 128), F32),
            pltpu.VMEM((4, 2, 256, 128), F32),
            pltpu.VMEM((4, 2, 272, 128), jnp.int16),
            pltpu.VMEM((4, 2, 272, 128), jnp.int16),
            pltpu.VMEM((4, 4, 4, 2, 5, 16, 128), jnp.int16),
            pltpu.VMEM((512, 128), F32),
            pltpu.VMEM((1024, 128), BF16),
            pltpu.VMEM((1024, 128), BF16),
            pltpu.VMEM((64, 1024), F32),
            pltpu.VMEM((64, 1024), F32),
            dma((16,)),
            dma((10,)),
            dma((8,)),
            dma((8,)),
            dma((10,)),
            dma((10,)),
            dma((27,)),
            dma((27,)),
            dma((4,)),
            dma((4,)),
        ],
        compiler_params=pltpu.CompilerParams(
            collective_id=0, has_side_effects=True, vmem_limit_bytes=62 * 1024 * 1024
        ),
        cost_estimate=pl.CostEstimate(
            flops=1200000000, bytes_accessed=20000000, transcendentals=0
        ),
    )(
        near_owner.T,
        near_slot.T,
        near_live.T,
        far_leaf,
        far_top,
        signal,
        leaf_basis,
        transfer,
        near_blocks,
        leaf_coupling,
        top_coupling,
    )


def solution(mesh):
    placed = (
        P(None, "surf"),
        P("surf", None, None, None),
        P("surf", None),
        P("surf", None),
        P("surf", None),
        P(None, "surf"),
        P("surf", None),
        P("surf", None, None),
        P("surf", None),
        P("surf", None, None),
        P("surf", None),
    )
    return jax.shard_map(
        shards, mesh=mesh, in_specs=placed, out_specs=P(None, "surf"), check_vma=False
    )
```

```python
import jax
import jax.numpy as jnp
from jax import lax
from jax.experimental import pallas as pl
from jax.experimental.pallas import tpu as pltpu
from jax.sharding import PartitionSpec as P

HOPS = 4
OFFS = 2 * HOPS + 1
LEAST = -24.0
STEPS = 800.0
MESH = pl.DeviceIdType.MESH
F32 = jnp.float32
BF16 = jnp.bfloat16
NT = (((1,), (1,)), ((), ()))


def split(value):
    high = value.astype(BF16)
    return high, (value - high.astype(F32)).astype(BF16)


def dot_two(value, matrix, dims=(((1,), (0,)), ((), ()))):
    high, low = split(value)
    return lax.dot_general(high, matrix, dims, preferred_element_type=F32) + lax.dot_general(
        low, matrix, dims, preferred_element_type=F32
    )


def encode(value):
    level = (jnp.log2(jnp.maximum(jnp.abs(value), 2.0**LEAST)) - LEAST) * STEPS
    level = jnp.round(jnp.minimum(level, 32767.0))
    return jnp.where(value < 0, -level, level).astype(jnp.int32).astype(jnp.int16)


def decode(level):
    size = jnp.exp2(jnp.abs(level) * (1.0 / STEPS) + LEAST)
    return jnp.where(level < 0, -size, jnp.where(level > 0, size, 0.0))


def kernel(
    owner_hbm,
    slot_hbm,
    live_hbm,
    far_leaf_hbm,
    far_top_hbm,
    signal_hbm,
    basis_hbm,
    transfer_hbm,
    near_hbm,
    leaf_hbm,
    top_hbm,
    out_ref,
    owner_ref,
    slot_ref,
    live_ref,
    far_leaf_ref,
    far_top_ref,
    signal_ref,
    basis_ref,
    transfer_ref,
    near_buf,
    leaf_buf,
    top_buf,
    window,
    outgoing,
    hot_rows,
    hot,
    even_terms,
    odd_terms,
    partner_terms,
    codes_out,
    codes_in,
    table,
    halves,
    tiles_0,
    tiles_1,
    tiles_2,
    tiles_3,
    tiles_4,
    sum_blocks,
    sum_children,
    leaf_acc,
    down_acc,
    near_sem,
    load_sem,
    sig_send,
    sig_recv,
    ret_send,
    ret_recv,
    tab_send,
    tab_recv,
    par_send,
    par_recv,
):
    rhs = 16
    leaf = 256
    clusters = 16
    near = 8
    n = 128
    me = lax.axis_index("surf")
    core = lax.rem(me, 2)
    y = lax.rem(me // 2, 4)
    z = lax.rem(me // 8, 4)
    x = me // 32

    def at(px, pz, py):
        return ((px * 4 + pz) * 4 + py) * 2 + core

    def turn(value, step):
        return lax.rem(value + step + 4, 4)

    def along(step):
        return lax.rem(me + step + n, n)

    partner = me + 1 - 2 * core
    steps = (1, -1, 2)
    y_peers = [at(x, z, turn(y, step)) for step in steps]
    z_peers = [at(x, turn(z, step), y) for step in steps]
    x_peers = [at(turn(x, step), z, y) for step in steps]
    surf_peers = [along(step) for step in (-4, -2, 2, 4)]

    loads = [
        pltpu.make_async_copy(src, dst, load_sem.at[i])
        for i, (src, dst) in enumerate(
            (
                (signal_hbm, signal_ref),
                (basis_hbm, basis_ref),
                (transfer_hbm, transfer_ref),
                (owner_hbm, owner_ref),
                (slot_hbm, slot_ref),
                (live_hbm, live_ref),
                (far_leaf_hbm, far_leaf_ref),
                (far_top_hbm, far_top_ref),
                (leaf_hbm, leaf_buf),
                (top_hbm, top_buf),
            )
        )
    ]
    near_in = [
        pltpu.make_async_copy(near_hbm.at[c], near_buf.at[c], near_sem.at[c])
        for c in range(clusters)
    ]
    for copy in loads[:3]:
        copy.start()
    barrier = pltpu.get_barrier_semaphore()
    peers = [partner] + surf_peers + y_peers + z_peers + x_peers
    for peer in peers:
        pl.semaphore_signal(barrier, inc=1, device_id=(peer,), device_id_type=MESH)
    for copy in loads[3:8] + near_in + loads[8:]:
        copy.start()

    group = lax.broadcasted_iota(jnp.int32, (rhs, 128), 1) // 32
    row_id = lax.broadcasted_iota(jnp.int32, (1024, 128), 0)
    lane_id = lax.broadcasted_iota(jnp.int32, (1024, 128), 1)
    sum_blocks[...] = (row_id // 32 == lane_id % 32).astype(F32).astype(BF16)
    sum_children[...] = (row_id % 32 == lane_id % 32).astype(F32).astype(BF16)

    loads[0].wait()
    for c in range(clusters):
        window[HOPS * clusters + c] = signal_ref[:, c * leaf : (c + 1) * leaf]

    pl.semaphore_wait(barrier, len(peers))

    def remote(src, dst, send, recv, device):
        return pltpu.make_async_remote_copy(
            src_ref=src,
            dst_ref=dst,
            send_sem=send,
            recv_sem=recv,
            device_id=(device,),
            device_id_type=MESH,
        )

    sent = []

    def start(copy):
        copy.start()
        sent.append(copy)
        return copy

    def arrived(copies):
        for copy in copies:
            copy.wait_recv()

    def tab(src, index, device):
        return start(remote(src, src, tab_send.at[index], tab_recv.at[index], device))

    def par(src, index):
        return start(remote(src, src, par_send.at[index], par_recv.at[index], partner))

    def place(offset):
        return window.at[pl.ds(offset * clusters, clusters)]

    def sig(src, dst, index, device):
        return start(remote(place(src), place(dst), sig_send.at[index], sig_recv.at[index], device))

    def moments():
        loads[1].wait()
        loads[2].wait()
        upper = jnp.zeros((rhs, 128), F32)
        for p in range(4):
            packed = jnp.zeros((rhs, 128), F32)
            lifted = [jnp.zeros((rhs, 128), F32) for _ in range(8)]
            for b in range(4):
                c = p * 4 + b
                columns = slice(c * leaf, (c + 1) * leaf)
                shape = basis_ref[:, columns]
                moment = lax.dot_general(
                    signal_ref[:, columns],
                    jnp.concatenate([shape] * 4, axis=0),
                    NT,
                    preferred_element_type=F32,
                )
                packed = jnp.where(group == b, moment, packed)
                lift = transfer_ref[c : c + 1, :]
                lifted = [a + moment * lift[:, g * 128 : (g + 1) * 128] for g, a in enumerate(lifted)]
            table[x, z, y, core, p] = encode(packed)
            total = dot_two(jnp.concatenate(lifted, axis=1), sum_blocks[...])
            upper = jnp.where(group == p, total, upper)
        table[x, z, y, core, 4] = encode(upper)

    lower, upper_half = pl.ds(0, 2), pl.ds(2, 2)

    def rows_along_y():
        own = table.at[x, z, y, core]
        return [tab(own, i, peer) for i, peer in enumerate(y_peers)]

    def halves_out(copies):
        arrived(copies)
        a = table.at[x, z, lower, core]
        b = table.at[x, z, upper_half, core]
        first = [tab(a, 3 + i, peer) for i, peer in enumerate(x_peers)]
        first += [tab(b, 6 + i, peer) for i, peer in enumerate(z_peers)]
        second = [tab(a, 9 + i, peer) for i, peer in enumerate(z_peers)]
        second += [tab(b, 12 + i, peer) for i, peer in enumerate(x_peers)]
        return first, second

    def halves_on(first, second):
        along_z, along_x = [], []
        for i, step in enumerate(steps):
            first[i].wait_recv()
            half = table.at[turn(x, -step), z, lower, core]
            along_z.append([tab(half, 15 + 3 * i + j, peer) for j, peer in enumerate(z_peers)])
            first[3 + i].wait_recv()
            half = table.at[x, turn(z, -step), upper_half, core]
            along_x.append([tab(half, 24 + 3 * i + j, peer) for j, peer in enumerate(x_peers)])
        return along_z, along_x, second

    def to_other_core(along_z, along_x, second):
        arrived(second[3:])
        copies = [par(table.at[:, z, :, core], 0)]
        for j, step in enumerate(steps):
            arrived([second[j]] + [row[j] for row in along_z] + along_x[j])
            copies.append(par(table.at[:, turn(z, -step), :, core], 1 + j))
        return copies

    window_row = lax.broadcasted_iota(jnp.int32, (1, 256), 1)

    def place_of(c, k):
        offset = lax.rem(owner_ref[k, c] - me + (HOPS + n), n)
        return jnp.minimum(offset, OFFS - 1) * clusters + slot_ref[k, c]

    def outward(first, count):
        @pl.loop(first, first + count)
        def _(c):
            pltpu.make_async_copy(near_hbm.at[c], near_buf.at[c], near_sem.at[c]).wait()
            here = signal_ref[:, pl.ds(pl.multiple_of(c * leaf, leaf), leaf)]
            for k in range(near):
                rows = pl.ds(pl.multiple_of((c * near + k) * rhs, rhs), rhs)
                term = jnp.dot(here, near_buf[c, k], preferred_element_type=F32)
                outgoing[0, rows, :] = term[:, :128]
                outgoing[1, rows, :] = term[:, 128:]
                target = place_of(c, k) + (1 - live_ref[k, c]) * 256
                hot_rows[pl.ds(c * near + k, 1), :] = jnp.where(window_row == target, 1.0, 0.0)

    def scatter(half):
        @pl.loop(0, rhs // 2)
        def _(pair):
            terms = jnp.concatenate(
                [
                    outgoing[half, pl.ds(pair * 2 + i, clusters * near, stride=rhs), :]
                    for i in range(2)
                ],
                axis=1,
            )
            high, low = split(terms)
            summed = jnp.dot(
                hot[...], jnp.concatenate([high, low], axis=0), preferred_element_type=F32
            )
            for i in range(2):
                rows = pl.ds(pl.multiple_of((pair * 2 + i) * clusters, clusters), clusters)
                for offset in range(OFFS):
                    terms_ref = odd_terms if offset % 2 else even_terms
                    terms_ref[offset // 2, half, rows, :] = summed[
                        offset * clusters : (offset + 1) * clusters, i * 128 : (i + 1) * 128
                    ]

    def ret(src, dst, index, device):
        return start(remote(src, dst, ret_send.at[index], ret_recv.at[index], device))

    def to_partner(half):
        return ret(odd_terms.at[:, half], partner_terms.at[:, half], 5 * half, partner)

    height = rhs * clusters

    def to_targets(half, copy):
        copy.wait_recv()
        copies = []
        for i, offset in enumerate((0, 1, 3, 4)):
            j = offset - 1 + core
            valid = jnp.logical_and(j >= 0, j <= 3)
            weight = jnp.where(valid, 1.0, 0.0)
            summed = (
                even_terms[offset, half]
                + partner_terms[jnp.clip(j, 0, 3), half] * weight
            )
            peak = jnp.maximum(jnp.max(jnp.abs(summed), keepdims=True), 2.0**-100)
            power = jnp.ceil(jnp.log2(peak * (1.0 / 32000.0)))
            codes_out[i, half, :height] = (
                jnp.round(summed * jnp.exp2(-power)).astype(jnp.int32).astype(jnp.int16)
            )
            codes_out[i, half, height:] = (
                jnp.broadcast_to(power, (16, 128)).astype(jnp.int32).astype(jnp.int16)
            )
            copies.append(
                ret(codes_out.at[i, half], codes_in.at[i, half], 5 * half + 1 + i, surf_peers[i])
            )
        even_terms[2, half] = even_terms[2, half] + partner_terms[1 + core, half]
        return copies

    def add_returned(half, copies):
        total = even_terms[2, half]
        for i, copy in enumerate(copies):
            copy.wait_recv()
            power = codes_in[i, half, height:].astype(jnp.int32).astype(F32)[:1]
            total = total + codes_in[i, half, :height].astype(jnp.int32).astype(F32) * jnp.exp2(
                power
            )
        even_terms[2, half] = total

    def inward(first, count):
        @pl.loop(first, first + count)
        def _(c):
            total = jnp.zeros((rhs, leaf), F32)
            for k in range(near):
                there = window[place_of(c, k)]
                there = (there.astype(F32) * live_ref[k, c].astype(F32)).astype(BF16)
                total = total + lax.dot_general(
                    there, near_buf[c, k], NT, preferred_element_type=F32
                )
            out_ref[:, pl.ds(pl.multiple_of(c * leaf, leaf), leaf)] = total

    def decode_plane(pz, pcore):
        @pl.loop(0, 16)
        def _(i):
            px, py = i // 4, i % 4
            for block in range(5):
                level = table[px, pz, py, pcore, block].astype(jnp.int32).astype(F32)
                high, low = split(decode(level))
                halves[(px * 32 + pz * 8 + py * 2 + pcore) * 5 + block] = jnp.concatenate(
                    [high, low], axis=1
                )

    pair_group = lax.broadcasted_iota(jnp.int32, (rhs, 256), 1) // 32 % 4

    def fetch(pick, tiles):
        for first in (0, 16):
            picked = []
            for k in range(first, first + 16):
                tile, quarter = pick(k)
                both = halves[tile]
                picked.append(jnp.where(pair_group == quarter, both, jnp.zeros_like(both)))
            tiles[first * rhs : (first + 16) * rhs, :] = jnp.dot(
                jnp.concatenate(picked, axis=0),
                sum_children[:256, :],
                preferred_element_type=F32,
            )

    def multiply(buf, row, tiles):
        sums = [jnp.zeros((rhs, 128), F32) for _ in range(8)]
        for eight in range(4):
            factors = buf[row, eight * 8 : eight * 8 + 8, :]
            for k in range(8):
                first = (eight * 8 + k) * rhs
                tile = tiles[first : first + rhs, :]
                sums = [
                    a + tile * factors[k : k + 1, g * 128 : (g + 1) * 128]
                    for g, a in enumerate(sums)
                ]
        return jnp.concatenate(sums, axis=1)

    def top_of(p):
        def pick(k):
            j = far_top_ref[p, k]
            return (j >> 2) * 5 + 4, j & 3

        return pick

    def leaf_of(c):
        def pick(k):
            j = far_leaf_ref[c, k]
            return (j >> 2) + (j >> 4), j & 3

        return pick

    def far():
        buffers = (tiles_0, tiles_1, tiles_2, tiles_3, tiles_4)
        fetch(top_of(0), buffers[0])

        @pl.loop(0, 4)
        def _(p):
            fetch(leaf_of(p * 4), buffers[1])
            top = dot_two(multiply(top_buf, p, buffers[0]), sum_blocks[...])[:, :32]
            spread = dot_two(top, sum_blocks[:, :32], NT)
            for b in range(4):
                c = p * 4 + b
                if b < 3:
                    fetch(leaf_of(c + 1), buffers[b + 2])
                else:
                    fetch(top_of(jnp.minimum(p + 1, 3)), buffers[0])
                rows = slice(b * rhs, (b + 1) * rhs)
                leaf_acc[rows, :] = multiply(leaf_buf, c, buffers[b + 1])
                down_acc[rows, :] = spread * transfer_ref[pl.ds(c, 1), :]
            field = dot_two(leaf_acc[...], sum_blocks[...]) + dot_two(
                down_acc[...], sum_children[...]
            )
            field = field[:, :32].astype(BF16)
            for b in range(4):
                columns = pl.ds(pl.multiple_of((p * 4 + b) * leaf, leaf), leaf)
                out_ref[:, columns] = out_ref[:, columns] + jnp.dot(
                    field[b * rhs : (b + 1) * rhs], basis_ref[:, columns], preferred_element_type=F32
                )

    signals = [
        sig(4, 6, 0, surf_peers[1]),
        sig(4, 2, 1, surf_peers[2]),
        sig(4, 8, 2, surf_peers[0]),
        sig(4, 0, 3, surf_peers[3]),
    ]
    pairs = [sig(4, 3 + 2 * core, 4, partner)]
    moments()
    legs = rows_along_y()
    for copy in loads[3:6]:
        copy.wait()
    outward(0, 16)
    legs = halves_out(legs)
    flipped = hot_rows[...].T.astype(BF16)
    hot[...] = jnp.concatenate([flipped, flipped], axis=1)[: OFFS * clusters, :]
    scatter(0)
    stage = [to_partner(0)]
    arrived(signals[:2])
    pairs += [sig(2, 1 + 2 * core, 5, partner), sig(6, 5 + 2 * core, 6, partner)]
    scatter(1)
    stage.append(to_partner(1))
    arrived(signals[2:])
    pairs.append(sig(8 - 8 * core, 7 - 6 * core, 7, partner))
    legs = halves_on(*legs)
    stage = [to_targets(half, copy) for half, copy in enumerate(stage)]
    for copy in loads[6:]:
        copy.wait()
    arrived(pairs)
    inward(0, 12)
    legs = to_other_core(*legs)
    inward(12, 4)
    for step in (0,) + steps:
        decode_plane(turn(z, -step), core)
    legs[0].wait_recv()
    decode_plane(z, 1 - core)
    for step, copy in zip(steps, legs[1:]):
        copy.wait_recv()
        decode_plane(turn(z, -step), 1 - core)
    far()
    for half, copies in enumerate(stage):
        add_returned(half, copies)

    @pl.loop(0, clusters)
    def _(c):
        rows = pl.ds(c, rhs, stride=clusters)
        for half in range(2):
            columns = pl.ds(pl.multiple_of(c * leaf + half * 128, 128), 128)
            out_ref[:, columns] = out_ref[:, columns] + even_terms[2, half, rows, :]

    for copy in sent:
        copy.wait_send()


def shards(
    signal,
    near_blocks,
    near_owner,
    near_slot,
    near_live,
    leaf_basis,
    transfer,
    leaf_coupling,
    far_leaf,
    top_coupling,
    far_top,
):
    hbm = pl.BlockSpec(memory_space=pl.ANY)
    dma = pltpu.SemaphoreType.DMA
    return pl.pallas_call(
        kernel,
        out_shape=jax.ShapeDtypeStruct((16, 4096), F32),
        in_specs=[hbm] * 11,
        out_specs=pl.BlockSpec(memory_space=pltpu.VMEM),
        scratch_shapes=[
            pltpu.SMEM((8, 16), jnp.int32),
            pltpu.SMEM((8, 16), jnp.int32),
            pltpu.SMEM((8, 16), jnp.int32),
            pltpu.SMEM((16, 32), jnp.int32),
            pltpu.SMEM((4, 32), jnp.int32),
            pltpu.VMEM((16, 4096), BF16),
            pltpu.VMEM((32, 4096), BF16),
            pltpu.VMEM((16, 1024), F32),
            pltpu.VMEM((16, 8, 256, 256), BF16),
            pltpu.VMEM((16, 32, 1024), F32),
            pltpu.VMEM((4, 32, 1024), F32),
            pltpu.VMEM((OFFS * 16, 16, 256), BF16),
            pltpu.VMEM((2, 2048, 128), F32),
            pltpu.VMEM((128, 256), F32),
            pltpu.VMEM((OFFS * 16, 256), BF16),
            pltpu.VMEM((5, 2, 256, 128), F32),
            pltpu.VMEM((4, 2, 256, 128), F32),
            pltpu.VMEM((4, 2, 256, 128), F32),
            pltpu.VMEM((4, 2, 272, 128), jnp.int16),
            pltpu.VMEM((4, 2, 272, 128), jnp.int16),
            pltpu.VMEM((4, 4, 4, 2, 5, 16, 128), jnp.int16),
            pltpu.VMEM((640, 16, 256), BF16),
            pltpu.VMEM((512, 128), F32),
            pltpu.VMEM((512, 128), F32),
            pltpu.VMEM((512, 128), F32),
            pltpu.VMEM((512, 128), F32),
            pltpu.VMEM((512, 128), F32),
            pltpu.VMEM((1024, 128), BF16),
            pltpu.VMEM((1024, 128), BF16),
            pltpu.VMEM((64, 1024), F32),
            pltpu.VMEM((64, 1024), F32),
            dma((16,)),
            dma((10,)),
            dma((8,)),
            dma((8,)),
            dma((10,)),
            dma((10,)),
            dma((33,)),
            dma((33,)),
            dma((4,)),
            dma((4,)),
        ],
        compiler_params=pltpu.CompilerParams(
            collective_id=0, has_side_effects=True, vmem_limit_bytes=62 * 1024 * 1024
        ),
        cost_estimate=pl.CostEstimate(
            flops=1200000000, bytes_accessed=20000000, transcendentals=0
        ),
    )(
        near_owner.T,
        near_slot.T,
        near_live.T,
        far_leaf,
        far_top,
        signal,
        leaf_basis,
        transfer,
        near_blocks,
        leaf_coupling,
        top_coupling,
    )


def solution(mesh):
    placed = (
        P(None, "surf"),
        P("surf", None, None, None),
        P("surf", None),
        P("surf", None),
        P("surf", None),
        P(None, "surf"),
        P("surf", None),
        P("surf", None, None),
        P("surf", None),
        P("surf", None, None),
        P("surf", None),
    )
    return jax.shard_map(
        shards, mesh=mesh, in_specs=placed, out_specs=P(None, "surf"), check_vma=False
    )
```

```python
import jax
import jax.numpy as jnp
from jax import lax
from jax.experimental import pallas as pl
from jax.experimental.pallas import tpu as pltpu
from jax.sharding import PartitionSpec as P

HOPS = 4
OFFS = 2 * HOPS + 1
LEAST = -24.0
STEPS = 800.0
MESH = pl.DeviceIdType.MESH
F32 = jnp.float32
BF16 = jnp.bfloat16
NT = (((1,), (1,)), ((), ()))


def split(value):
    high = value.astype(BF16)
    return high, (value - high.astype(F32)).astype(BF16)


def dot_two(value, matrix, dims=(((1,), (0,)), ((), ()))):
    high, low = split(value)
    return lax.dot_general(high, matrix, dims, preferred_element_type=F32) + lax.dot_general(
        low, matrix, dims, preferred_element_type=F32
    )


def encode(value):
    level = (jnp.log2(jnp.maximum(jnp.abs(value), 2.0**LEAST)) - LEAST) * STEPS
    level = jnp.round(jnp.minimum(level, 32767.0))
    return jnp.where(value < 0, -level, level).astype(jnp.int32).astype(jnp.int16)


def decode(level):
    size = jnp.exp2(jnp.abs(level) * (1.0 / STEPS) + LEAST)
    return jnp.where(level < 0, -size, jnp.where(level > 0, size, 0.0))


def kernel(
    owner_hbm,
    slot_hbm,
    live_hbm,
    far_leaf_hbm,
    far_top_hbm,
    signal_hbm,
    basis_hbm,
    transfer_hbm,
    near_hbm,
    leaf_hbm,
    top_hbm,
    out_ref,
    owner_ref,
    slot_ref,
    live_ref,
    far_leaf_ref,
    far_top_ref,
    signal_ref,
    basis_ref,
    transfer_ref,
    near_buf,
    leaf_buf,
    top_buf,
    window,
    outgoing,
    hot_rows,
    hot,
    even_terms,
    odd_terms,
    partner_terms,
    codes_out,
    codes_in,
    table,
    halves,
    tiles_0,
    tiles_1,
    tiles_2,
    tiles_3,
    tiles_4,
    sum_blocks,
    sum_children,
    leaf_acc,
    down_acc,
    near_sem,
    load_sem,
    sig_send,
    sig_recv,
    ret_send,
    ret_recv,
    tab_send,
    tab_recv,
    par_send,
    par_recv,
):
    rhs = 16
    leaf = 256
    clusters = 16
    near = 8
    n = 128
    me = lax.axis_index("surf")
    core = lax.rem(me, 2)
    y = lax.rem(me // 2, 4)
    z = lax.rem(me // 8, 4)
    x = me // 32

    def at(px, pz, py):
        return ((px * 4 + pz) * 4 + py) * 2 + core

    def turn(value, step):
        return lax.rem(value + step + 4, 4)

    def along(step):
        return lax.rem(me + step + n, n)

    partner = me + 1 - 2 * core
    steps = (1, -1, 2)
    y_peers = [at(x, z, turn(y, step)) for step in steps]
    z_peers = [at(x, turn(z, step), y) for step in steps]
    x_peers = [at(turn(x, step), z, y) for step in steps]
    surf_peers = [along(step) for step in (-4, -2, 2, 4)]

    loads = [
        pltpu.make_async_copy(src, dst, load_sem.at[i])
        for i, (src, dst) in enumerate(
            (
                (signal_hbm, signal_ref),
                (basis_hbm, basis_ref),
                (transfer_hbm, transfer_ref),
                (owner_hbm, owner_ref),
                (slot_hbm, slot_ref),
                (live_hbm, live_ref),
                (far_leaf_hbm, far_leaf_ref),
                (far_top_hbm, far_top_ref),
                (leaf_hbm, leaf_buf),
                (top_hbm, top_buf),
            )
        )
    ]
    near_in = [
        pltpu.make_async_copy(near_hbm.at[c], near_buf.at[c], near_sem.at[c])
        for c in range(clusters)
    ]
    for copy in loads[:3]:
        copy.start()
    barrier = pltpu.get_barrier_semaphore()
    peers = [partner] + surf_peers + y_peers + z_peers + x_peers
    for peer in peers:
        pl.semaphore_signal(barrier, inc=1, device_id=(peer,), device_id_type=MESH)
    for copy in loads[3:8] + near_in + loads[8:]:
        copy.start()

    group = lax.broadcasted_iota(jnp.int32, (rhs, 128), 1) // 32
    row_id = lax.broadcasted_iota(jnp.int32, (1024, 128), 0)
    lane_id = lax.broadcasted_iota(jnp.int32, (1024, 128), 1)
    sum_blocks[...] = (row_id // 32 == lane_id % 32).astype(F32).astype(BF16)
    sum_children[...] = (row_id % 32 == lane_id % 32).astype(F32).astype(BF16)

    loads[0].wait()
    for c in range(clusters):
        window[HOPS * clusters + c] = signal_ref[:, c * leaf : (c + 1) * leaf]

    pl.semaphore_wait(barrier, len(peers))

    def remote(src, dst, send, recv, device):
        return pltpu.make_async_remote_copy(
            src_ref=src,
            dst_ref=dst,
            send_sem=send,
            recv_sem=recv,
            device_id=(device,),
            device_id_type=MESH,
        )

    sent = []

    def start(copy):
        copy.start()
        sent.append(copy)
        return copy

    def arrived(copies):
        for copy in copies:
            copy.wait_recv()

    def tab(src, index, device):
        return start(remote(src, src, tab_send.at[index], tab_recv.at[index], device))

    def par(src, index):
        return start(remote(src, src, par_send.at[index], par_recv.at[index], partner))

    def place(offset):
        return window.at[pl.ds(offset * clusters, clusters)]

    def sig(src, dst, index, device):
        return start(remote(place(src), place(dst), sig_send.at[index], sig_recv.at[index], device))

    def moments():
        loads[1].wait()
        loads[2].wait()
        upper = jnp.zeros((rhs, 128), F32)
        for p in range(4):
            packed = jnp.zeros((rhs, 128), F32)
            lifted = [jnp.zeros((rhs, 128), F32) for _ in range(8)]
            for b in range(4):
                c = p * 4 + b
                columns = slice(c * leaf, (c + 1) * leaf)
                shape = basis_ref[:, columns]
                moment = lax.dot_general(
                    signal_ref[:, columns],
                    jnp.concatenate([shape] * 4, axis=0),
                    NT,
                    preferred_element_type=F32,
                )
                packed = jnp.where(group == b, moment, packed)
                lift = transfer_ref[c : c + 1, :]
                lifted = [a + moment * lift[:, g * 128 : (g + 1) * 128] for g, a in enumerate(lifted)]
            table[x, z, y, core, p] = encode(packed)
            total = dot_two(jnp.concatenate(lifted, axis=1), sum_blocks[...])
            upper = jnp.where(group == p, total, upper)
        table[x, z, y, core, 4] = encode(upper)

    lower, upper_half = pl.ds(0, 2), pl.ds(2, 2)

    def rows_along_y():
        own = table.at[x, z, y, core]
        return [tab(own, i, peer) for i, peer in enumerate(y_peers)]

    def halves_out(copies):
        arrived(copies)
        a = table.at[x, z, lower, core]
        b = table.at[x, z, upper_half, core]
        first = [tab(a, 3 + i, peer) for i, peer in enumerate(x_peers)]
        first += [tab(b, 6 + i, peer) for i, peer in enumerate(z_peers)]
        second = [tab(a, 9 + i, peer) for i, peer in enumerate(z_peers)]
        second += [tab(b, 12 + i, peer) for i, peer in enumerate(x_peers)]
        return first, second

    def halves_on(first, second):
        along_z, along_x = [], []
        for i, step in enumerate(steps):
            first[i].wait_recv()
            half = table.at[turn(x, -step), z, lower, core]
            along_z.append([tab(half, 15 + 3 * i + j, peer) for j, peer in enumerate(z_peers)])
            first[3 + i].wait_recv()
            half = table.at[x, turn(z, -step), upper_half, core]
            along_x.append([tab(half, 24 + 3 * i + j, peer) for j, peer in enumerate(x_peers)])
        return along_z, along_x, second

    def to_other_core(along_z, along_x, second):
        arrived(second[3:])
        copies = [par(table.at[:, z, :, core], 0)]
        for j, step in enumerate(steps):
            arrived([second[j]] + [row[j] for row in along_z] + along_x[j])
            copies.append(par(table.at[:, turn(z, -step), :, core], 1 + j))
        return copies

    window_row = lax.broadcasted_iota(jnp.int32, (1, 256), 1)

    def place_of(c, k):
        offset = lax.rem(owner_ref[k, c] - me + (HOPS + n), n)
        return jnp.minimum(offset, OFFS - 1) * clusters + slot_ref[k, c]

    def outward(first, count):
        @pl.loop(first, first + count)
        def _(c):
            pltpu.make_async_copy(near_hbm.at[c], near_buf.at[c], near_sem.at[c]).wait()
            here = signal_ref[:, pl.ds(pl.multiple_of(c * leaf, leaf), leaf)]
            for k in range(near):
                rows = pl.ds(pl.multiple_of((c * near + k) * rhs, rhs), rhs)
                term = jnp.dot(here, near_buf[c, k], preferred_element_type=F32)
                outgoing[0, rows, :] = term[:, :128]
                outgoing[1, rows, :] = term[:, 128:]
                target = place_of(c, k) + (1 - live_ref[k, c]) * 256
                hot_rows[pl.ds(c * near + k, 1), :] = jnp.where(window_row == target, 1.0, 0.0)

    def scatter(half):
        @pl.loop(0, rhs // 2)
        def _(pair):
            terms = jnp.concatenate(
                [
                    outgoing[half, pl.ds(pair * 2 + i, clusters * near, stride=rhs), :]
                    for i in range(2)
                ],
                axis=1,
            )
            high, low = split(terms)
            summed = jnp.dot(
                hot[...], jnp.concatenate([high, low], axis=0), preferred_element_type=F32
            )
            for i in range(2):
                rows = pl.ds(pl.multiple_of((pair * 2 + i) * clusters, clusters), clusters)
                for offset in range(OFFS):
                    terms_ref = odd_terms if offset % 2 else even_terms
                    terms_ref[offset // 2, half, rows, :] = summed[
                        offset * clusters : (offset + 1) * clusters, i * 128 : (i + 1) * 128
                    ]

    def ret(src, dst, index, device):
        return start(remote(src, dst, ret_send.at[index], ret_recv.at[index], device))

    def to_partner(half):
        return ret(odd_terms.at[:, half], partner_terms.at[:, half], 5 * half, partner)

    height = rhs * clusters

    def to_targets(half, copy):
        copy.wait_recv()
        copies = []
        for i, offset in enumerate((0, 1, 3, 4)):
            j = offset - 1 + core
            valid = jnp.logical_and(j >= 0, j <= 3)
            weight = jnp.where(valid, 1.0, 0.0)
            summed = (
                even_terms[offset, half]
                + partner_terms[jnp.clip(j, 0, 3), half] * weight
            )
            peak = jnp.maximum(jnp.max(jnp.abs(summed), keepdims=True), 2.0**-100)
            power = jnp.ceil(jnp.log2(peak * (1.0 / 32000.0)))
            codes_out[i, half, :height] = (
                jnp.round(summed * jnp.exp2(-power)).astype(jnp.int32).astype(jnp.int16)
            )
            codes_out[i, half, height:] = (
                jnp.broadcast_to(power, (16, 128)).astype(jnp.int32).astype(jnp.int16)
            )
            copies.append(
                ret(codes_out.at[i, half], codes_in.at[i, half], 5 * half + 1 + i, surf_peers[i])
            )
        even_terms[2, half] = even_terms[2, half] + partner_terms[1 + core, half]
        return copies

    def add_returned(half, copies):
        total = even_terms[2, half]
        for i, copy in enumerate(copies):
            copy.wait_recv()
            power = codes_in[i, half, height:].astype(jnp.int32).astype(F32)[:1]
            total = total + codes_in[i, half, :height].astype(jnp.int32).astype(F32) * jnp.exp2(
                power
            )
        even_terms[2, half] = total

    def inward(first, count):
        @pl.loop(first, first + count)
        def _(c):
            total = jnp.zeros((rhs, leaf), F32)
            for k in range(near):
                there = window[place_of(c, k)]
                there = (there.astype(F32) * live_ref[k, c].astype(F32)).astype(BF16)
                total = total + lax.dot_general(
                    there, near_buf[c, k], NT, preferred_element_type=F32
                )
            out_ref[:, pl.ds(pl.multiple_of(c * leaf, leaf), leaf)] = total

    def decode_plane(pz, pcore):
        @pl.loop(0, 16)
        def _(i):
            px, py = i // 4, i % 4
            for block in range(5):
                level = table[px, pz, py, pcore, block].astype(jnp.int32).astype(F32)
                high, low = split(decode(level))
                halves[(px * 32 + pz * 8 + py * 2 + pcore) * 5 + block] = jnp.concatenate(
                    [high, low], axis=1
                )

    pair_group = lax.broadcasted_iota(jnp.int32, (rhs, 256), 1) // 32 % 4

    def fetch(pick, tiles):
        for first in (0, 16):
            picked = []
            for k in range(first, first + 16):
                tile, quarter = pick(k)
                both = halves[tile]
                picked.append(jnp.where(pair_group == quarter, both, jnp.zeros_like(both)))
            tiles[first * rhs : (first + 16) * rhs, :] = jnp.dot(
                jnp.concatenate(picked, axis=0),
                sum_children[:256, :],
                preferred_element_type=F32,
            )

    def multiply(buf, row, tiles):
        sums = [jnp.zeros((rhs, 128), F32) for _ in range(8)]
        for eight in range(4):
            for k in range(8):
                first = (eight * 8 + k) * rhs
                tile = tiles[first : first + rhs, :]
                sums = [
                    a + tile * buf[row, eight * 8 + k : eight * 8 + k + 1, g * 128 : (g + 1) * 128]
                    for g, a in enumerate(sums)
                ]
        return jnp.concatenate(sums, axis=1)

    def top_of(p):
        def pick(k):
            j = far_top_ref[p, k]
            return (j >> 2) * 5 + 4, j & 3

        return pick

    def leaf_of(c):
        def pick(k):
            j = far_leaf_ref[c, k]
            return (j >> 2) + (j >> 4), j & 3

        return pick

    def far():
        buffers = (tiles_0, tiles_1, tiles_2, tiles_3, tiles_4)
        fetch(top_of(0), buffers[0])

        @pl.loop(0, 4)
        def _(p):
            fetch(leaf_of(p * 4), buffers[1])
            top = dot_two(multiply(top_buf, p, buffers[0]), sum_blocks[...])[:, :32]
            spread = dot_two(top, sum_blocks[:, :32], NT)
            for b in range(4):
                c = p * 4 + b
                if b < 3:
                    fetch(leaf_of(c + 1), buffers[b + 2])
                else:
                    fetch(top_of(jnp.minimum(p + 1, 3)), buffers[0])
                rows = slice(b * rhs, (b + 1) * rhs)
                leaf_acc[rows, :] = multiply(leaf_buf, c, buffers[b + 1])
                down_acc[rows, :] = spread * transfer_ref[pl.ds(c, 1), :]
            field = dot_two(leaf_acc[...], sum_blocks[...]) + dot_two(
                down_acc[...], sum_children[...]
            )
            field = field[:, :32].astype(BF16)
            for b in range(4):
                columns = pl.ds(pl.multiple_of((p * 4 + b) * leaf, leaf), leaf)
                out_ref[:, columns] = out_ref[:, columns] + jnp.dot(
                    field[b * rhs : (b + 1) * rhs], basis_ref[:, columns], preferred_element_type=F32
                )

    signals = [
        sig(4, 6, 0, surf_peers[1]),
        sig(4, 2, 1, surf_peers[2]),
        sig(4, 8, 2, surf_peers[0]),
        sig(4, 0, 3, surf_peers[3]),
    ]
    pairs = [sig(4, 3 + 2 * core, 4, partner)]
    moments()
    legs = rows_along_y()
    for copy in loads[3:6]:
        copy.wait()
    outward(0, 16)
    legs = halves_out(legs)
    flipped = hot_rows[...].T.astype(BF16)
    hot[...] = jnp.concatenate([flipped, flipped], axis=1)[: OFFS * clusters, :]
    scatter(0)
    stage = [to_partner(0)]
    arrived(signals[:2])
    pairs += [sig(2, 1 + 2 * core, 5, partner), sig(6, 5 + 2 * core, 6, partner)]
    scatter(1)
    stage.append(to_partner(1))
    arrived(signals[2:])
    pairs.append(sig(8 - 8 * core, 7 - 6 * core, 7, partner))
    legs = halves_on(*legs)
    for copy in loads[6:]:
        copy.wait()
    arrived(pairs)
    inward(0, 12)
    stage = [to_targets(half, copy) for half, copy in enumerate(stage)]
    legs = to_other_core(*legs)
    inward(12, 4)
    for step in (0,) + steps:
        decode_plane(turn(z, -step), core)
    legs[0].wait_recv()
    decode_plane(z, 1 - core)
    for step, copy in zip(steps, legs[1:]):
        copy.wait_recv()
        decode_plane(turn(z, -step), 1 - core)
    far()
    for half, copies in enumerate(stage):
        add_returned(half, copies)

    @pl.loop(0, clusters)
    def _(c):
        rows = pl.ds(c, rhs, stride=clusters)
        for half in range(2):
            columns = pl.ds(pl.multiple_of(c * leaf + half * 128, 128), 128)
            out_ref[:, columns] = out_ref[:, columns] + even_terms[2, half, rows, :]

    for copy in sent:
        copy.wait_send()


def shards(
    signal,
    near_blocks,
    near_owner,
    near_slot,
    near_live,
    leaf_basis,
    transfer,
    leaf_coupling,
    far_leaf,
    top_coupling,
    far_top,
):
    hbm = pl.BlockSpec(memory_space=pl.ANY)
    dma = pltpu.SemaphoreType.DMA
    return pl.pallas_call(
        kernel,
        out_shape=jax.ShapeDtypeStruct((16, 4096), F32),
        in_specs=[hbm] * 11,
        out_specs=pl.BlockSpec(memory_space=pltpu.VMEM),
        scratch_shapes=[
            pltpu.SMEM((8, 16), jnp.int32),
            pltpu.SMEM((8, 16), jnp.int32),
            pltpu.SMEM((8, 16), jnp.int32),
            pltpu.SMEM((16, 32), jnp.int32),
            pltpu.SMEM((4, 32), jnp.int32),
            pltpu.VMEM((16, 4096), BF16),
            pltpu.VMEM((32, 4096), BF16),
            pltpu.VMEM((16, 1024), F32),
            pltpu.VMEM((16, 8, 256, 256), BF16),
            pltpu.VMEM((16, 32, 1024), F32),
            pltpu.VMEM((4, 32, 1024), F32),
            pltpu.VMEM((OFFS * 16, 16, 256), BF16),
            pltpu.VMEM((2, 2048, 128), F32),
            pltpu.VMEM((128, 256), F32),
            pltpu.VMEM((OFFS * 16, 256), BF16),
            pltpu.VMEM((5, 2, 256, 128), F32),
            pltpu.VMEM((4, 2, 256, 128), F32),
            pltpu.VMEM((4, 2, 256, 128), F32),
            pltpu.VMEM((4, 2, 272, 128), jnp.int16),
            pltpu.VMEM((4, 2, 272, 128), jnp.int16),
            pltpu.VMEM((4, 4, 4, 2, 5, 16, 128), jnp.int16),
            pltpu.VMEM((640, 16, 256), BF16),
            pltpu.VMEM((512, 128), F32),
            pltpu.VMEM((512, 128), F32),
            pltpu.VMEM((512, 128), F32),
            pltpu.VMEM((512, 128), F32),
            pltpu.VMEM((512, 128), F32),
            pltpu.VMEM((1024, 128), BF16),
            pltpu.VMEM((1024, 128), BF16),
            pltpu.VMEM((64, 1024), F32),
            pltpu.VMEM((64, 1024), F32),
            dma((16,)),
            dma((10,)),
            dma((8,)),
            dma((8,)),
            dma((10,)),
            dma((10,)),
            dma((33,)),
            dma((33,)),
            dma((4,)),
            dma((4,)),
        ],
        compiler_params=pltpu.CompilerParams(
            collective_id=0, has_side_effects=True, vmem_limit_bytes=62 * 1024 * 1024
        ),
        cost_estimate=pl.CostEstimate(
            flops=1200000000, bytes_accessed=20000000, transcendentals=0
        ),
    )(
        near_owner.T,
        near_slot.T,
        near_live.T,
        far_leaf,
        far_top,
        signal,
        leaf_basis,
        transfer,
        near_blocks,
        leaf_coupling,
        top_coupling,
    )


def solution(mesh):
    placed = (
        P(None, "surf"),
        P("surf", None, None, None),
        P("surf", None),
        P("surf", None),
        P("surf", None),
        P(None, "surf"),
        P("surf", None),
        P("surf", None, None),
        P("surf", None),
        P("surf", None, None),
        P("surf", None),
    )
    return jax.shard_map(
        shards, mesh=mesh, in_specs=placed, out_specs=P(None, "surf"), check_vma=False
    )
```
